256 devices in a mesh: depth: 32 (over z, x), row: 4 (over y), col: 2 (over core).
Axes of the slice: x: 4, y: 4, z: 8, core: 2. Of those that a mesh axis runs over, the one named last changes fastest.
Arguments:
- tokens: bfloat16 [2048, 6144], P(('depth', 'col'), 'row'), may hold values from -16 to 16
- w_in: bfloat16 [6144, 12288], P('row', 'depth'), may hold values from -0.078125 to 0.078125
- w_out: bfloat16 [12288, 6144], P('depth', 'row'), may hold values from -0.0546875 to 0.0546875
- cotangent: bfloat16 [2048, 6144], P(('depth', 'col'), 'row'), may hold values from -2.5 to 2.5
Outputs:
- mixed: bfloat16 [2048, 6144], P(('depth', 'col'), 'row')
- grad_tokens: bfloat16 [2048, 6144], P(('depth', 'col'), 'row')
- grad_w_in: bfloat16 [6144, 12288], P('row', 'depth')
- grad_w_out: bfloat16 [12288, 6144], P('depth', 'row')
The draws below stay inside these ranges and needn't reach their ends.
All inputs are finite; a program needn't handle non-finite values.
Results may differ from the reference program's by a relative error of at most 0.027.
Values may be sent and summed in bfloat16 or wider, within the bound.
No kernel may reach another device: no remote copies, remote signals or barrier semaphores. Data moves between devices by JAX's collectives and lax.ppermute only.
A program may use at most 64 MiB of HBM per device.

```python
import jax
import jax.numpy as jnp
from jax import lax

D = 6144
FF = 12288
TOK_DEV = 32
TOKENS = 2048
N_DEPTH = 32
N_ROW = 4
N_COL = 2


def raised(entries, key, source, target, blocks, factor):
    def block_of(position):
        return (jnp.arange(entries.shape[position]) // (entries.shape[position] // blocks)).reshape((-1,) + (1,) * (entries.ndim - 1 - position))

    near = jax.random.permutation(key, blocks)[block_of(target)]
    second = (block_of(target) + blocks // 2) % blocks
    return jnp.where((block_of(source) == near) | (block_of(source) == second), factor * entries, entries)


def block_scale(own_key, extent, pieces, smallest, top_value):
    level = 1.0
    for dim, parts in pieces:
        heights = jax.random.uniform(jax.random.fold_in(jax.random.fold_in(own_key, 6), dim), (parts,), jnp.float32, smallest / len(pieces), top_value / len(pieces))
        level = level * jnp.repeat(jnp.exp(heights), extent[dim] // parts).reshape((-1,) + (1,) * (len(extent) - 1 - dim))
    return level


def bell_draw(rng, dims, spread, most, cuts=(), kind=jnp.bfloat16):
    result = jax.random.normal(rng, dims, jnp.float32) * spread
    if len(cuts) > 0:
        result = block_scale(rng, dims, cuts, -0.22, 0.18) * result
    return jnp.clip(result, min=-most, max=most).astype(kind)


def noise_with(own_key, shape, width, most, shards, heavy, held_as=jnp.bfloat16):
    array = width * jax.random.normal(own_key, shape, jnp.float32)
    if shards:
        array = array * block_scale(own_key, shape, shards, -0.22, 0.18)
    return jnp.clip(raised(array, jax.random.fold_in(own_key, 3), *heavy), -most, most).astype(held_as)


def setup_inputs(seed: int = 0) -> dict:
    key_list = jax.random.split(jax.random.key(seed), 5)
    return {
        "tokens": noise_with(key_list[0], (TOKENS, D), 1.0, 16.0, ((0, 64), (1, 4)), (1, 0, 64, 4.0)),
        "w_in": bell_draw(key_list[1], (D, FF), D ** -0.5, 0.078125, ((0, 4), (1, 32))),
        "w_out": bell_draw(key_list[2], (FF, D), FF ** -0.5, 0.0546875, ((0, 32), (1, 4))),
        "cotangent": noise_with(key_list[3], (TOKENS, D), (TOKENS ** -0.25), 2.5, ((0, 64), (1, 4)), (1, 0, 64, 4.0)),
    }


root_half = 0.7071067811865476
inv_root_two_pi = 0.3989422804014327


def gelu_value(pre_act):
    return pre_act * 0.5 * (1.0 + lax.erf(pre_act * root_half))


def gelu_slope(pre_act):
    return 0.5 * (1.0 + lax.erf(pre_act * root_half)) + pre_act * jnp.exp(-0.5 * pre_act * pre_act) * inv_root_two_pi


def rounded_blocks(left_side, right_side, blocks):
    block_width = left_side.shape[1] // blocks
    running = jnp.zeros((left_side.shape[0], right_side.shape[1]), jnp.float32)
    for piece_index in range(blocks):
        lower = piece_index * block_width
        upper = lower + block_width
        product = jnp.dot(left_side[:, lower:upper], right_side[lower:upper], preferred_element_type=jnp.float32)
        running = running + lax.optimization_barrier(product.astype(jnp.bfloat16)).astype(jnp.float32)
    return running


def group_sum(first, second):
    first_blocks = first.reshape(N_DEPTH, N_COL, TOK_DEV, first.shape[1])
    second_blocks = second.reshape(N_DEPTH, N_COL, TOK_DEV, second.shape[1])
    running = jnp.zeros((first.shape[1], second.shape[1]), jnp.float32)
    for group in range(N_COL):
        left_rows = first_blocks[:, group].reshape(N_DEPTH * TOK_DEV, first.shape[1])
        right_rows = second_blocks[:, group].reshape(N_DEPTH * TOK_DEV, second.shape[1])
        product = lax.dot_general(left_rows, right_rows, (((0,), (0,)), ((), ())), preferred_element_type=jnp.float32)
        running = running + lax.optimization_barrier(product.astype(jnp.bfloat16)).astype(jnp.float32)
    return running.astype(jnp.bfloat16)


def reference(tokens, w_in, w_out, cotangent):
    pre_act = rounded_blocks(tokens, w_in, N_ROW)
    hidden = gelu_value(pre_act).astype(jnp.bfloat16)
    mixed = jnp.dot(hidden, w_out, preferred_element_type=jnp.float32).astype(jnp.bfloat16)
    grad_hidden = rounded_blocks(cotangent, w_out.T, N_ROW)
    grad_pre = (grad_hidden * gelu_slope(pre_act)).astype(jnp.bfloat16)
    grad_tokens = jnp.dot(grad_pre, w_in.T, preferred_element_type=jnp.float32).astype(jnp.bfloat16)
    grad_w_in = group_sum(tokens, grad_pre)
    grad_w_out = group_sum(hidden, cotangent)
    return mixed, grad_tokens, grad_w_in, grad_w_out
```

```python
import jax
import jax.numpy as jnp
from jax import lax
from jax.experimental import pallas as pl
from jax.experimental.pallas import tpu as pltpu
from jax.sharding import PartitionSpec as P

root_half = 0.7071067811865476
inv_root_two_pi = 0.3989422804014327
NZ, NX, NY, NC = 8, 4, 4, 2
bf16 = jnp.bfloat16
f32 = jnp.float32


def gelu_value(pre_act):
    return pre_act * 0.5 * (1.0 + lax.erf(pre_act * root_half))


def gelu_slope(pre_act):
    return (
        0.5 * (1.0 + lax.erf(pre_act * root_half))
        + pre_act * jnp.exp(-0.5 * pre_act * pre_act) * inv_root_two_pi
    )


def shift_zx(value, core0, core1):
    pairs = []
    for z in range(NZ):
        for x in range(NX):
            for c, off in enumerate((core0, core1)):
                if off is not None:
                    to = ((z + off[0]) % NZ) * NX + (x + off[1]) % NX
                    pairs.append(((z * NX + x) * NC + c, to * NC + c))
    return lax.ppermute(value, ("depth", "col"), pairs)


def shift_y(value, core0, core1):
    pairs = []
    for y in range(NY):
        for c, off in enumerate((core0, core1)):
            pairs.append((y * NC + c, ((y + off) % NY) * NC + c))
    return lax.ppermute(value, ("row", "col"), pairs)


def swap(value):
    return lax.ppermute(value, "col", [(0, 1), (1, 0)])


def cat(parts):
    return jnp.concatenate(parts, axis=0)


def add(*terms):
    total = terms[0].astype(f32)
    for t in terms[1:]:
        total = total + t.astype(f32)
    return total


def ring_zx(value, dz, dx):
    return shift_zx(value, (dz, dx), (-dz, -dx))


VMEM = pl.BlockSpec(memory_space=pltpu.VMEM)
SMEM = pl.BlockSpec(memory_space=pltpu.SMEM)


def join(parts):
    arrays = []
    for a, _, _ in parts:
        if not any(a is other for other in arrays):
            arrays.append(a)
    places = [next(i for i, other in enumerate(arrays) if other is a) for a, _, _ in parts]
    rows = sum(t - s for _, s, t in parts)
    width = arrays[0].shape[1]

    def kernel(*refs):
        at = 0
        for i, (_, s, t) in zip(places, parts):
            refs[-1][at : at + t - s, :] = refs[i][s:t, :]
            at += t - s

    return pl.pallas_call(
        kernel,
        out_shape=jax.ShapeDtypeStruct((rows, width), bf16),
        in_specs=[VMEM] * len(arrays),
        out_specs=VMEM,
        compiler_params=pltpu.CompilerParams(vmem_limit_bytes=16 * 2**20),
        cost_estimate=pl.CostEstimate(
            flops=0, bytes_accessed=4 * rows * width, transcendentals=0
        ),
    )(*arrays)


def whole(*arrays):
    return join([(a, 0, a.shape[0]) for a in arrays])


def together(*values):
    return lax.optimization_barrier(values)


def gather(a, b):
    w, a = together(whole(b, swap(b)), a)
    s1 = ring_zx(w, 1, 0)
    s2 = ring_zx(w, 2, 0)
    vu = ring_zx(a, 0, 1)
    vd = ring_zx(a, 0, -1)
    v2 = ring_zx(a, 0, 2)
    own = whole(a, vu, vd, v2)
    so = swap(own)
    o1 = ring_zx(own, 1, 0)
    so, h1, h2 = together(so, whole(b, s1, s2), join([(s1, 0, 64), (s2, 0, 32)]))
    x1 = ring_zx(so, 1, 0)
    o2 = ring_zx(o1, 1, 0)
    u1 = ring_zx(h1, 0, 1)
    d1 = ring_zx(h1, 0, -1)
    h2 = ring_zx(h2, 2, 0)
    x2 = ring_zx(x1, 1, 0)
    o3 = ring_zx(o2, 1, 0)
    f1 = ring_zx(u1, 0, 1)
    u2 = ring_zx(h2, 0, 1)
    d2 = ring_zx(h2, 0, -1)
    x3 = ring_zx(x2, 1, 0)
    o4 = ring_zx(o3, 1, 0)
    f2 = ring_zx(u2, 0, 1)
    return whole(own, o1, x1, o2, x2, o3, x3, o4), whole(h1, h2, u1, u2, d1, d2, f1, f2)


def scatter(part_a, part_b, weight_grads):
    own, o1, x1, o2, x2, o3, x3, o4 = (part_a[128 * j : 128 * (j + 1)] for j in range(8))
    h1, u1, d1, f1 = (part_b[256 * j : 256 * j + 160] for j in range(4))
    h2, u2, d2, f2 = (part_b[256 * j + 160 : 256 * (j + 1)] for j in range(4))
    q = ring_zx(o4.astype(bf16), -1, 0)
    p = ring_zx(x3.astype(bf16), -1, 0)
    f2 = ring_zx(f2.astype(bf16), 0, -1)
    f1 = ring_zx(f1.astype(bf16), 0, -1)
    q, p, d2, d1 = together(
        add(o3, q).astype(bf16), add(x2, p).astype(bf16), d2.astype(bf16), d1.astype(bf16)
    )
    q = ring_zx(q, -1, 0)
    p = ring_zx(p, -1, 0)
    d2 = ring_zx(d2, 0, 1)
    d1 = ring_zx(d1, 0, 1)
    q, p, u2, u1 = together(
        add(o2, q).astype(bf16),
        add(x1, p).astype(bf16),
        add(u2, f2).astype(bf16),
        add(u1, f1).astype(bf16),
    )
    q = ring_zx(q, -1, 0)
    p = ring_zx(p, -1, 0)
    grads = weight_grads(u1)
    u2 = ring_zx(u2, 0, -1)
    u1 = ring_zx(u1, 0, -1)
    q, p, t = together(add(o1, q).astype(bf16), p, add(h2, u2, d2).astype(bf16))
    t = ring_zx(t, -2, 0)
    q = ring_zx(q, -1, 0)
    p = swap(p)
    own = add(own, q, p)
    h1 = add(h1, u1, d1)
    vu, vd, v2, s1, s2, *grads = together(
        own[32:64].astype(bf16),
        own[64:96].astype(bf16),
        own[96:].astype(bf16),
        add(h1[32:96], t[:64]).astype(bf16),
        cat([add(h1[96:128], t[64:]), h1[128:]]).astype(bf16),
        *grads,
    )
    s1 = ring_zx(s1, -1, 0)
    s2 = ring_zx(s2, -2, 0)
    vu = ring_zx(vu, 0, -1)
    vd = ring_zx(vd, 0, 1)
    v2 = ring_zx(v2, 0, -2)
    last = swap(add(s1[32:], s2[32:]).astype(bf16))
    out_a = add(own[:32], vu, vd, v2).astype(bf16)
    out_b = add(h1[:32], s1[:32], s2[:32], last).astype(bf16)
    return out_a, out_b, *grads


def local(kernel, out_shapes, row, *arrays):
    size = 2 * sum(a.size * a.dtype.itemsize for a in arrays)
    return pl.pallas_call(
        kernel,
        out_shape=out_shapes,
        in_specs=[SMEM] + [VMEM] * len(arrays),
        out_specs=jax.tree.map(lambda _: VMEM, out_shapes),
        compiler_params=pltpu.CompilerParams(vmem_limit_bytes=16 * 2**20),
        cost_estimate=pl.CostEstimate(flops=0, bytes_accessed=size, transcendentals=0),
    )(row.reshape(1), *arrays)


CHUNK = jax.ShapeDtypeStruct((256, 384), bf16)


OTHER = (2, 4, 6)


def chunks_a(row, part):
    def kernel(where, ref, *outs):
        for o, out in enumerate(outs):
            x = lax.rem(where[0] + o, NY)
            crossed = jnp.where((x == 1) | (x == 2), 3 - x, x)
            for g in range(8):
                at = pl.multiple_of(128 * g + 32 * (crossed if g in OTHER else x), 32)
                out[32 * g : 32 * (g + 1), :] = ref[pl.ds(at, 32), :]

    return local(kernel, [CHUNK] * 4, row, part)


def chunks_b(row, part):
    def kernel(where, ref, *outs):
        for o, out in enumerate(outs):
            at = pl.multiple_of(lax.rem(where[0] + o, NY) * 256, 256)
            out[...] = ref[pl.ds(at, 256), :]

    return local(kernel, [CHUNK] * 4, row, part)


def join_b(row, parts):
    def kernel(where, *refs):
        for o in range(NY):
            at = pl.multiple_of(lax.rem(where[0] + o, NY) * 256, 256)
            refs[4][pl.ds(at, 256), :] = refs[o][...]

    return local(kernel, jax.ShapeDtypeStruct((1024, 384), bf16), row, *parts)


def join_a(row, parts):
    def kernel(where, *refs):
        for o in range(NY):
            x = lax.rem(where[0] + o, NY)
            crossed = jnp.where((x == 1) | (x == 2), 3 - x, x)
            for g in range(8):
                refs[4][g, crossed if g in OTHER else x] = refs[o][32 * g : 32 * (g + 1), :]

    out = local(kernel, jax.ShapeDtypeStruct((8, 4, 32, 384), bf16), row, *parts)
    return out.reshape(1024, 384)


def scatter_y(at):
    far = shift_y(at[2], 2, -2)
    up = shift_y(at[1], 1, 1)
    down = shift_y(at[3], -1, -1)
    return add(at[0], up, down, far)


def gather_y(mine):
    far = shift_y(mine, 2, -2)
    below = shift_y(mine, 1, 1)
    above = shift_y(mine, -1, -1)
    return [mine, above, far, below]


def dot(left, right, dims):
    return lax.dot_general(left, right, ((dims[:1], dims[1:]), ((), ())), preferred_element_type=f32)


def on_device(tokens, w_in, w_out, cotangent):
    row = lax.axis_index("row")
    cot_rows, tok_rows = gather(cotangent, tokens)
    pre = scatter_y(chunks_b(row, dot(tok_rows, w_in, (1, 0)).astype(bf16)))
    hidden, pre = together(gelu_value(pre).astype(bf16), pre)
    hidden_rows = join_a(row, gather_y(hidden))
    part_mixed = dot(hidden_rows, w_out, (1, 0))
    grad_hidden = scatter_y(chunks_a(row, dot(cot_rows, w_out, (1, 1)).astype(bf16)))
    grad_pre = (grad_hidden * gelu_slope(pre)).astype(bf16)
    pre_grad_rows = join_b(row, gather_y(grad_pre))
    part_tokens = dot(pre_grad_rows, w_in, (1, 1))

    def weight_grads(early):
        hidden_late, pre_grad_late, _ = together(hidden_rows, pre_grad_rows, early)
        part_in = dot(tok_rows, pre_grad_late, (0, 0)).astype(bf16)
        part_out = dot(hidden_late, cot_rows, (0, 0)).astype(bf16)
        return add(part_in, swap(part_in)).astype(bf16), add(part_out, swap(part_out)).astype(bf16)

    return scatter(part_mixed, part_tokens, weight_grads)


def solution(mesh):
    placed = (
        P(("depth", "col"), "row"),
        P("row", "depth"),
        P("depth", "row"),
        P(("depth", "col"), "row"),
    )
    return jax.shard_map(
        on_device,
        mesh=mesh,
        in_specs=placed,
        out_specs=(
            P(("depth", "col"), "row"),
            P(("depth", "col"), "row"),
            P("row", "depth"),
            P("depth", "row"),
        ),
        check_vma=False,
    )
```

```python
import jax
import jax.numpy as jnp
from jax import lax
from jax.experimental import pallas as pl
from jax.experimental.pallas import tpu as pltpu
from jax.sharding import PartitionSpec as P

root_half = 0.7071067811865476
inv_root_two_pi = 0.3989422804014327
NZ, NX, NY, NC = 8, 4, 4, 2
bf16 = jnp.bfloat16
f32 = jnp.float32


def gelu_value(pre_act):
    return pre_act * 0.5 * (1.0 + lax.erf(pre_act * root_half))


def gelu_slope(pre_act):
    return (
        0.5 * (1.0 + lax.erf(pre_act * root_half))
        + pre_act * jnp.exp(-0.5 * pre_act * pre_act) * inv_root_two_pi
    )


def shift_zx(value, core0, core1):
    pairs = []
    for z in range(NZ):
        for x in range(NX):
            for c, off in enumerate((core0, core1)):
                if off is not None:
                    to = ((z + off[0]) % NZ) * NX + (x + off[1]) % NX
                    pairs.append(((z * NX + x) * NC + c, to * NC + c))
    return lax.ppermute(value, ("depth", "col"), pairs)


def shift_y(value, core0, core1):
    pairs = []
    for y in range(NY):
        for c, off in enumerate((core0, core1)):
            pairs.append((y * NC + c, ((y + off) % NY) * NC + c))
    return lax.ppermute(value, ("row", "col"), pairs)


def swap(value):
    return lax.ppermute(value, "col", [(0, 1), (1, 0)])


def cat(parts):
    return jnp.concatenate(parts, axis=0)


def add(*terms):
    total = terms[0].astype(f32)
    for t in terms[1:]:
        total = total + t.astype(f32)
    return total


def ring_zx(value, dz, dx):
    return shift_zx(value, (dz, dx), (-dz, -dx))


VMEM = pl.BlockSpec(memory_space=pltpu.VMEM)
SMEM = pl.BlockSpec(memory_space=pltpu.SMEM)


def join(parts):
    arrays = []
    for a, _, _ in parts:
        if not any(a is other for other in arrays):
            arrays.append(a)
    places = [next(i for i, other in enumerate(arrays) if other is a) for a, _, _ in parts]
    rows = sum(t - s for _, s, t in parts)
    width = arrays[0].shape[1]

    def kernel(*refs):
        at = 0
        for i, (_, s, t) in zip(places, parts):
            refs[-1][at : at + t - s, :] = refs[i][s:t, :]
            at += t - s

    return pl.pallas_call(
        kernel,
        out_shape=jax.ShapeDtypeStruct((rows, width), bf16),
        in_specs=[VMEM] * len(arrays),
        out_specs=VMEM,
        compiler_params=pltpu.CompilerParams(vmem_limit_bytes=16 * 2**20),
        cost_estimate=pl.CostEstimate(
            flops=0, bytes_accessed=4 * rows * width, transcendentals=0
        ),
    )(*arrays)


def whole(*arrays):
    return join([(a, 0, a.shape[0]) for a in arrays])


def together(*values):
    return lax.optimization_barrier(values)


def gather(a, b):
    w, a = together(whole(b, swap(b)), a)
    s1 = ring_zx(w, 1, 0)
    s2 = ring_zx(w, 2, 0)
    vu = ring_zx(a, 0, 1)
    vd = ring_zx(a, 0, -1)
    v2 = ring_zx(a, 0, 2)
    own = whole(a, vu, vd, v2)
    so = swap(own)
    o1 = ring_zx(own, 1, 0)
    so, h1, h2 = together(so, whole(b, s1, s2), join([(s1, 0, 64), (s2, 0, 32)]))
    x1 = ring_zx(so, 1, 0)
    o2 = ring_zx(o1, 1, 0)
    u1 = ring_zx(h1, 0, 1)
    d1 = ring_zx(h1, 0, -1)
    h2 = ring_zx(h2, 2, 0)
    x2 = ring_zx(x1, 1, 0)
    o3 = ring_zx(o2, 1, 0)
    f1 = ring_zx(u1, 0, 1)
    u2 = ring_zx(h2, 0, 1)
    d2 = ring_zx(h2, 0, -1)
    x3 = ring_zx(x2, 1, 0)
    o4 = ring_zx(o3, 1, 0)
    f2 = ring_zx(u2, 0, 1)
    return whole(own, o1, x1, o2, x2, o3, x3, o4), whole(h1, h2, u1, u2, d1, d2, f1, f2)


def scatter(part_a, part_b, weight_grads):
    own, o1, x1, o2, x2, o3, x3, o4 = (part_a[128 * j : 128 * (j + 1)] for j in range(8))
    h1, u1, d1, f1 = (part_b[256 * j : 256 * j + 160] for j in range(4))
    h2, u2, d2, f2 = (part_b[256 * j + 160 : 256 * (j + 1)] for j in range(4))
    q = ring_zx(o4.astype(bf16), -1, 0)
    p = ring_zx(x3.astype(bf16), -1, 0)
    f2 = ring_zx(f2.astype(bf16), 0, -1)
    f1 = ring_zx(f1.astype(bf16), 0, -1)
    q, d2, d1, x2 = together(add(o3, q).astype(bf16), d2.astype(bf16), d1.astype(bf16), x2)
    parts = weight_grads(f1)
    swapped = [swap(part) for part in parts]
    q = ring_zx(q, -1, 0)
    d2 = ring_zx(d2, 0, 1)
    d1 = ring_zx(d1, 0, 1)
    p, o2 = together(add(x2, p).astype(bf16), o2)
    p = ring_zx(p, -1, 0)
    q, u2, u1, x1, *parts = together(
        add(o2, q).astype(bf16),
        add(u2, f2).astype(bf16),
        add(u1, f1).astype(bf16),
        x1,
        *parts,
        *swapped,
    )
    q = ring_zx(q, -1, 0)
    u2 = ring_zx(u2, 0, -1)
    u1 = ring_zx(u1, 0, -1)
    p, o1 = together(add(x1, p).astype(bf16), o1)
    p = ring_zx(p, -1, 0)
    u2, *parts = together(u2, *parts)
    grads = [add(part, other).astype(bf16) for part, other in zip(parts[:2], parts[2:])]
    o1, *grads = together(o1, *grads)
    q = ring_zx(add(o1, q).astype(bf16), -1, 0)
    t = ring_zx(add(h2, u2, d2).astype(bf16), -2, 0)
    p = swap(p)
    own = add(own, q, p)
    vu, vd, v2, h1 = together(
        own[32:64].astype(bf16), own[64:96].astype(bf16), own[96:].astype(bf16), add(h1, u1, d1)
    )
    s1 = add(h1[32:96], t[:64]).astype(bf16)
    s2 = cat([add(h1[96:128], t[64:]), h1[128:]]).astype(bf16)
    s1 = ring_zx(s1, -1, 0)
    s2 = ring_zx(s2, -2, 0)
    vu = ring_zx(vu, 0, -1)
    vd = ring_zx(vd, 0, 1)
    v2 = ring_zx(v2, 0, -2)
    last = swap(add(s1[32:], s2[32:]).astype(bf16))
    out_a = add(own[:32], vu, vd, v2).astype(bf16)
    out_b = add(h1[:32], s1[:32], s2[:32], last).astype(bf16)
    return out_a, out_b, *grads


def local(kernel, out_shapes, row, *arrays):
    size = 2 * sum(a.size * a.dtype.itemsize for a in arrays)
    return pl.pallas_call(
        kernel,
        out_shape=out_shapes,
        in_specs=[SMEM] + [VMEM] * len(arrays),
        out_specs=jax.tree.map(lambda _: VMEM, out_shapes),
        compiler_params=pltpu.CompilerParams(vmem_limit_bytes=16 * 2**20),
        cost_estimate=pl.CostEstimate(flops=0, bytes_accessed=size, transcendentals=0),
    )(row.reshape(1), *arrays)


CHUNK = jax.ShapeDtypeStruct((256, 384), bf16)


OTHER = (2, 4, 6)


def chunks_a(row, part):
    def kernel(where, ref, *outs):
        for o, out in enumerate(outs):
            x = lax.rem(where[0] + o, NY)
            crossed = jnp.where((x == 1) | (x == 2), 3 - x, x)
            for g in range(8):
                at = pl.multiple_of(128 * g + 32 * (crossed if g in OTHER else x), 32)
                out[32 * g : 32 * (g + 1), :] = ref[pl.ds(at, 32), :]

    return local(kernel, [CHUNK] * 4, row, part)


def chunks_b(row, part):
    def kernel(where, ref, *outs):
        for o, out in enumerate(outs):
            at = pl.multiple_of(lax.rem(where[0] + o, NY) * 256, 256)
            out[...] = ref[pl.ds(at, 256), :]

    return local(kernel, [CHUNK] * 4, row, part)


def join_b(row, parts):
    def kernel(where, *refs):
        for o in range(NY):
            at = pl.multiple_of(lax.rem(where[0] + o, NY) * 256, 256)
            refs[4][pl.ds(at, 256), :] = refs[o][...]

    return local(kernel, jax.ShapeDtypeStruct((1024, 384), bf16), row, *parts)


def join_a(row, parts):
    def kernel(where, *refs):
        for o in range(NY):
            x = lax.rem(where[0] + o, NY)
            crossed = jnp.where((x == 1) | (x == 2), 3 - x, x)
            for g in range(8):
                refs[4][g, crossed if g in OTHER else x] = refs[o][32 * g : 32 * (g + 1), :]

    out = local(kernel, jax.ShapeDtypeStruct((8, 4, 32, 384), bf16), row, *parts)
    return out.reshape(1024, 384)


def scatter_y(at):
    far = shift_y(at[2], 2, -2)
    up = shift_y(at[1], 1, 1)
    down = shift_y(at[3], -1, -1)
    return add(at[0], up, down, far)


def gather_y(mine):
    far = shift_y(mine, 2, -2)
    below = shift_y(mine, 1, 1)
    above = shift_y(mine, -1, -1)
    return [mine, above, far, below]


def dot(left, right, dims):
    return lax.dot_general(left, right, ((dims[:1], dims[1:]), ((), ())), preferred_element_type=f32)


def on_device(tokens, w_in, w_out, cotangent):
    row = lax.axis_index("row")
    cot_rows, tok_rows = gather(cotangent, tokens)
    pre = scatter_y(chunks_b(row, dot(tok_rows, w_in, (1, 0)).astype(bf16)))
    hidden, pre = together(gelu_value(pre).astype(bf16), pre)
    hidden_rows = join_a(row, gather_y(hidden))
    part_mixed = dot(hidden_rows, w_out, (1, 0))
    grad_hidden = scatter_y(chunks_a(row, dot(cot_rows, w_out, (1, 1)).astype(bf16)))
    grad_pre = (grad_hidden * gelu_slope(pre)).astype(bf16)
    pre_grad_rows = join_b(row, gather_y(grad_pre))
    part_tokens = dot(pre_grad_rows, w_in, (1, 1))

    def weight_grads(early):
        hidden_late, pre_grad_late, _ = together(hidden_rows, pre_grad_rows, early)
        return (
            dot(tok_rows, pre_grad_late, (0, 0)).astype(bf16),
            dot(hidden_late, cot_rows, (0, 0)).astype(bf16),
        )

    return scatter(part_mixed, part_tokens, weight_grads)


def solution(mesh):
    placed = (
        P(("depth", "col"), "row"),
        P("row", "depth"),
        P("depth", "row"),
        P(("depth", "col"), "row"),
    )
    return jax.shard_map(
        on_device,
        mesh=mesh,
        in_specs=placed,
        out_specs=(
            P(("depth", "col"), "row"),
            P(("depth", "col"), "row"),
            P("row", "depth"),
            P("depth", "row"),
        ),
        check_vma=False,
    )
```

```python
import jax
import jax.numpy as jnp
from jax import lax
from jax.experimental import pallas as pl
from jax.experimental.pallas import tpu as pltpu
from jax.sharding import PartitionSpec as P

root_half = 0.7071067811865476
inv_root_two_pi = 0.3989422804014327
NZ, NX, NY, NC = 8, 4, 4, 2
bf16 = jnp.bfloat16
f32 = jnp.float32


def gelu_value(pre_act):
    return pre_act * 0.5 * (1.0 + lax.erf(pre_act * root_half))


def gelu_slope(pre_act):
    return (
        0.5 * (1.0 + lax.erf(pre_act * root_half))
        + pre_act * jnp.exp(-0.5 * pre_act * pre_act) * inv_root_two_pi
    )


def shift_zx(value, core0, core1):
    pairs = []
    for z in range(NZ):
        for x in range(NX):
            for c, off in enumerate((core0, core1)):
                if off is not None:
                    to = ((z + off[0]) % NZ) * NX + (x + off[1]) % NX
                    pairs.append(((z * NX + x) * NC + c, to * NC + c))
    return lax.ppermute(value, ("depth", "col"), pairs)


def shift_y(value, core0, core1):
    pairs = []
    for y in range(NY):
        for c, off in enumerate((core0, core1)):
            pairs.append((y * NC + c, ((y + off) % NY) * NC + c))
    return lax.ppermute(value, ("row", "col"), pairs)


def swap(value):
    return lax.ppermute(value, "col", [(0, 1), (1, 0)])


def cat(parts):
    return jnp.concatenate(parts, axis=0)


def add(*terms):
    total = terms[0].astype(f32)
    for t in terms[1:]:
        total = total + t.astype(f32)
    return total


def ring_zx(value, dz, dx):
    return shift_zx(value, (dz, dx), (-dz, -dx))


VMEM = pl.BlockSpec(memory_space=pltpu.VMEM)
SMEM = pl.BlockSpec(memory_space=pltpu.SMEM)


def join(parts):
    arrays = []
    for a, _, _ in parts:
        if not any(a is other for other in arrays):
            arrays.append(a)
    places = [next(i for i, other in enumerate(arrays) if other is a) for a, _, _ in parts]
    rows = sum(t - s for _, s, t in parts)
    width = arrays[0].shape[1]

    def kernel(*refs):
        at = 0
        for i, (_, s, t) in zip(places, parts):
            refs[-1][at : at + t - s, :] = refs[i][s:t, :]
            at += t - s

    return pl.pallas_call(
        kernel,
        out_shape=jax.ShapeDtypeStruct((rows, width), bf16),
        in_specs=[VMEM] * len(arrays),
        out_specs=VMEM,
        compiler_params=pltpu.CompilerParams(vmem_limit_bytes=16 * 2**20),
        cost_estimate=pl.CostEstimate(
            flops=0, bytes_accessed=4 * rows * width, transcendentals=0
        ),
    )(*arrays)


def whole(*arrays):
    return join([(a, 0, a.shape[0]) for a in arrays])


def together(*values):
    return lax.optimization_barrier(values)


def gather(a, b):
    w, a = together(whole(b, swap(b)), a)
    s1 = ring_zx(w, 1, 0)
    s2 = ring_zx(w, 2, 0)
    vu = ring_zx(a, 0, 1)
    vd = ring_zx(a, 0, -1)
    v2 = ring_zx(a, 0, 2)
    own, s1, s2 = together(whole(a, vu, vd, v2), s1, s2)
    so = swap(own)
    o1 = ring_zx(own, 1, 0)
    h1 = whole(b, s1, s2)
    h2 = join([(s1, 0, 64), (s2, 0, 32)])
    x1 = ring_zx(so, 1, 0)
    o2 = ring_zx(o1, 1, 0)
    u1 = ring_zx(h1, 0, 1)
    d1 = ring_zx(h1, 0, -1)
    h2 = ring_zx(h2, 2, 0)
    x2 = ring_zx(x1, 1, 0)
    o3 = ring_zx(o2, 1, 0)
    f1 = ring_zx(u1, 0, 1)
    u2 = ring_zx(h2, 0, 1)
    d2 = ring_zx(h2, 0, -1)
    x3 = ring_zx(x2, 1, 0)
    o4 = ring_zx(o3, 1, 0)
    f2 = ring_zx(u2, 0, 1)
    return whole(own, o1, x1, o2, x2, o3, x3, o4), whole(h1, h2, u1, u2, d1, d2, f1, f2)


def scatter(part_a, part_b, weight_grads):
    own, o1, x1, o2, x2, o3, x3, o4 = (part_a[128 * j : 128 * (j + 1)] for j in range(8))
    h1, u1, d1, f1 = (part_b[256 * j : 256 * j + 160] for j in range(4))
    h2, u2, d2, f2 = (part_b[256 * j + 160 : 256 * (j + 1)] for j in range(4))
    q = ring_zx(o4.astype(bf16), -1, 0)
    p = ring_zx(x3.astype(bf16), -1, 0)
    f2 = ring_zx(f2.astype(bf16), 0, -1)
    f1 = ring_zx(f1.astype(bf16), 0, -1)
    q, d2, d1, x2 = together(add(o3, q).astype(bf16), d2.astype(bf16), d1.astype(bf16), x2)
    parts = weight_grads(f1)
    swapped = [swap(part) for part in parts]
    q = ring_zx(q, -1, 0)
    d2 = ring_zx(d2, 0, 1)
    d1 = ring_zx(d1, 0, 1)
    p, o2 = together(add(x2, p).astype(bf16), o2)
    p = ring_zx(p, -1, 0)
    q, u2, u1, x1, *parts = together(
        add(o2, q).astype(bf16),
        add(u2, f2).astype(bf16),
        add(u1, f1).astype(bf16),
        x1,
        *parts,
        *swapped,
    )
    q = ring_zx(q, -1, 0)
    u2 = ring_zx(u2, 0, -1)
    u1 = ring_zx(u1, 0, -1)
    p, o1 = together(add(x1, p).astype(bf16), o1)
    p = ring_zx(p, -1, 0)
    u1, *parts = together(u1, *parts)
    grads = [add(part, other).astype(bf16) for part, other in zip(parts[:2], parts[2:])]
    q = ring_zx(add(o1, q).astype(bf16), -1, 0)
    t = ring_zx(add(h2, u2, d2).astype(bf16), -2, 0)
    p, *grads = together(swap(p), *grads)
    own = add(own, q, p)
    vu, vd, v2, h1 = together(
        own[32:64].astype(bf16), own[64:96].astype(bf16), own[96:].astype(bf16), add(h1, u1, d1)
    )
    s1 = add(h1[32:96], t[:64]).astype(bf16)
    s2 = cat([add(h1[96:128], t[64:]), h1[128:]]).astype(bf16)
    s1 = ring_zx(s1, -1, 0)
    s2 = ring_zx(s2, -2, 0)
    vu = ring_zx(vu, 0, -1)
    vd = ring_zx(vd, 0, 1)
    v2 = ring_zx(v2, 0, -2)
    last = swap(add(s1[32:], s2[32:]).astype(bf16))
    out_a = add(own[:32], vu, vd, v2).astype(bf16)
    out_b = add(h1[:32], s1[:32], s2[:32], last).astype(bf16)
    return out_a, out_b, *grads


def local(kernel, out_shapes, row, *arrays):
    size = 2 * sum(a.size * a.dtype.itemsize for a in arrays)
    return pl.pallas_call(
        kernel,
        out_shape=out_shapes,
        in_specs=[SMEM] + [VMEM] * len(arrays),
        out_specs=jax.tree.map(lambda _: VMEM, out_shapes),
        compiler_params=pltpu.CompilerParams(vmem_limit_bytes=16 * 2**20),
        cost_estimate=pl.CostEstimate(flops=0, bytes_accessed=size, transcendentals=0),
    )(row.reshape(1), *arrays)


CHUNK = jax.ShapeDtypeStruct((256, 384), bf16)


OTHER = (2, 4, 6)


def chunks_a(row, part):
    def kernel(where, ref, *outs):
        for o, out in enumerate(outs):
            x = lax.rem(where[0] + o, NY)
            crossed = jnp.where((x == 1) | (x == 2), 3 - x, x)
            for g in range(8):
                at = pl.multiple_of(128 * g + 32 * (crossed if g in OTHER else x), 32)
                out[32 * g : 32 * (g + 1), :] = ref[pl.ds(at, 32), :]

    return local(kernel, [CHUNK] * 4, row, part)


def chunks_b(row, part):
    def kernel(where, ref, *outs):
        for o, out in enumerate(outs):
            at = pl.multiple_of(lax.rem(where[0] + o, NY) * 256, 256)
            out[...] = ref[pl.ds(at, 256), :]

    return local(kernel, [CHUNK] * 4, row, part)


def join_b(row, parts):
    def kernel(where, *refs):
        for o in range(NY):
            at = pl.multiple_of(lax.rem(where[0] + o, NY) * 256, 256)
            refs[4][pl.ds(at, 256), :] = refs[o][...]

    return local(kernel, jax.ShapeDtypeStruct((1024, 384), bf16), row, *parts)


def join_a(row, parts):
    def kernel(where, *refs):
        for o in range(NY):
            x = lax.rem(where[0] + o, NY)
            crossed = jnp.where((x == 1) | (x == 2), 3 - x, x)
            for g in range(8):
                refs[4][g, crossed if g in OTHER else x] = refs[o][32 * g : 32 * (g + 1), :]

    out = local(kernel, jax.ShapeDtypeStruct((8, 4, 32, 384), bf16), row, *parts)
    return out.reshape(1024, 384)


def scatter_y(at):
    far = shift_y(at[2], 2, -2)
    up = shift_y(at[1], 1, 1)
    down = shift_y(at[3], -1, -1)
    return add(at[0], up, down, far)


def gather_y(mine):
    far = shift_y(mine, 2, -2)
    below = shift_y(mine, 1, 1)
    above = shift_y(mine, -1, -1)
    return [mine, above, far, below]


def dot(left, right, dims):
    return lax.dot_general(left, right, ((dims[:1], dims[1:]), ((), ())), preferred_element_type=f32)


def on_device(tokens, w_in, w_out, cotangent):
    row = lax.axis_index("row")
    cot_rows, tok_rows = gather(cotangent, tokens)
    pre = scatter_y(chunks_b(row, dot(tok_rows, w_in, (1, 0)).astype(bf16)))
    hidden, pre = together(gelu_value(pre).astype(bf16), pre)
    hidden_rows = join_a(row, gather_y(hidden))
    part_mixed = dot(hidden_rows, w_out, (1, 0))
    grad_hidden = scatter_y(chunks_a(row, dot(cot_rows, w_out, (1, 1)).astype(bf16)))
    grad_pre = (grad_hidden * gelu_slope(pre)).astype(bf16)
    pre_grad_rows = join_b(row, gather_y(grad_pre))
    part_tokens = dot(pre_grad_rows, w_in, (1, 1))

    def weight_grads(early):
        hidden_late, pre_grad_late, _ = together(hidden_rows, pre_grad_rows, early)
        return (
            dot(tok_rows, pre_grad_late, (0, 0)).astype(bf16),
            dot(hidden_late, cot_rows, (0, 0)).astype(bf16),
        )

    return scatter(part_mixed, part_tokens, weight_grads)


def solution(mesh):
    placed = (
        P(("depth", "col"), "row"),
        P("row", "depth"),
        P("depth", "row"),
        P(("depth", "col"), "row"),
    )
    return jax.shard_map(
        on_device,
        mesh=mesh,
        in_specs=placed,
        out_specs=(
            P(("depth", "col"), "row"),
            P(("depth", "col"), "row"),
            P("row", "depth"),
            P("depth", "row"),
        ),
        check_vma=False,
    )
```

```python
import jax
import jax.numpy as jnp
from jax import lax
from jax.experimental import pallas as pl
from jax.experimental.pallas import tpu as pltpu
from jax.sharding import PartitionSpec as P

root_half = 0.7071067811865476
inv_root_two_pi = 0.3989422804014327
NZ, NX, NY, NC = 8, 4, 4, 2
bf16 = jnp.bfloat16
f32 = jnp.float32


def gelu_value(pre_act):
    return pre_act * 0.5 * (1.0 + lax.erf(pre_act * root_half))


def gelu_slope(pre_act):
    return (
        0.5 * (1.0 + lax.erf(pre_act * root_half))
        + pre_act * jnp.exp(-0.5 * pre_act * pre_act) * inv_root_two_pi
    )


def shift_zx(value, core0, core1):
    pairs = []
    for z in range(NZ):
        for x in range(NX):
            for c, off in enumerate((core0, core1)):
                if off is not None:
                    to = ((z + off[0]) % NZ) * NX + (x + off[1]) % NX
                    pairs.append(((z * NX + x) * NC + c, to * NC + c))
    return lax.ppermute(value, ("depth", "col"), pairs)


def shift_y(value, core0, core1):
    pairs = []
    for y in range(NY):
        for c, off in enumerate((core0, core1)):
            pairs.append((y * NC + c, ((y + off) % NY) * NC + c))
    return lax.ppermute(value, ("row", "col"), pairs)


def swap(value):
    return lax.ppermute(value, "col", [(0, 1), (1, 0)])


def cat(parts):
    return jnp.concatenate(parts, axis=0)


def add(*terms):
    total = terms[0].astype(f32)
    for t in terms[1:]:
        total = total + t.astype(f32)
    return total


def ring_zx(value, dz, dx):
    return shift_zx(value, (dz, dx), (-dz, -dx))


VMEM = pl.BlockSpec(memory_space=pltpu.VMEM)
SMEM = pl.BlockSpec(memory_space=pltpu.SMEM)


def join(parts):
    arrays = []
    for a, _, _ in parts:
        if not any(a is other for other in arrays):
            arrays.append(a)
    places = [next(i for i, other in enumerate(arrays) if other is a) for a, _, _ in parts]
    rows = sum(t - s for _, s, t in parts)
    width = arrays[0].shape[1]

    def kernel(*refs):
        at = 0
        for i, (_, s, t) in zip(places, parts):
            refs[-1][at : at + t - s, :] = refs[i][s:t, :]
            at += t - s

    return pl.pallas_call(
        kernel,
        out_shape=jax.ShapeDtypeStruct((rows, width), bf16),
        in_specs=[VMEM] * len(arrays),
        out_specs=VMEM,
        compiler_params=pltpu.CompilerParams(vmem_limit_bytes=16 * 2**20),
        cost_estimate=pl.CostEstimate(
            flops=0, bytes_accessed=4 * rows * width, transcendentals=0
        ),
    )(*arrays)


def whole(*arrays):
    return join([(a, 0, a.shape[0]) for a in arrays])


def together(*values):
    return lax.optimization_barrier(values)


def gather(a, b):
    w, a = together(whole(b, swap(b)), a)
    s1 = ring_zx(w, 1, 0)
    s2 = ring_zx(w, 2, 0)
    vu = ring_zx(a, 0, 1)
    vd = ring_zx(a, 0, -1)
    v2 = ring_zx(a, 0, 2)
    own, s1, s2 = together(whole(a, vu, vd, v2), s1, s2)
    so = swap(own)
    o1 = ring_zx(own, 1, 0)
    so, h1, h2 = together(so, whole(b, s1, s2), join([(s1, 0, 64), (s2, 0, 32)]))
    x1 = ring_zx(so, 1, 0)
    o2 = ring_zx(o1, 1, 0)
    u1 = ring_zx(h1, 0, 1)
    d1 = ring_zx(h1, 0, -1)
    h2 = ring_zx(h2, 2, 0)
    x2 = ring_zx(x1, 1, 0)
    o3 = ring_zx(o2, 1, 0)
    f1 = ring_zx(u1, 0, 1)
    u2 = ring_zx(h2, 0, 1)
    d2 = ring_zx(h2, 0, -1)
    x3 = ring_zx(x2, 1, 0)
    o4 = ring_zx(o3, 1, 0)
    f2 = ring_zx(u2, 0, 1)
    return whole(own, o1, x1, o2, x2, o3, x3, o4), whole(h1, h2, u1, u2, d1, d2, f1, f2)


def scatter(part_a, part_b, weight_grads):
    own, o1, x1, o2, x2, o3, x3, o4 = (part_a[128 * j : 128 * (j + 1)] for j in range(8))
    h1, u1, d1, f1 = (part_b[256 * j : 256 * j + 160] for j in range(4))
    h2, u2, d2, f2 = (part_b[256 * j + 160 : 256 * (j + 1)] for j in range(4))
    q = ring_zx(o4.astype(bf16), -1, 0)
    p = ring_zx(x3.astype(bf16), -1, 0)
    f2 = ring_zx(f2.astype(bf16), 0, -1)
    f1 = ring_zx(f1.astype(bf16), 0, -1)
    q, d2, d1, x2 = together(add(o3, q).astype(bf16), d2.astype(bf16), d1.astype(bf16), x2)
    parts = weight_grads(f1)
    swapped = [swap(part) for part in parts]
    q = ring_zx(q, -1, 0)
    d2 = ring_zx(d2, 0, 1)
    d1 = ring_zx(d1, 0, 1)
    p, o2 = together(add(x2, p).astype(bf16), o2)
    p = ring_zx(p, -1, 0)
    q, u2, u1, x1, *parts = together(
        add(o2, q).astype(bf16),
        add(u2, f2).astype(bf16),
        add(u1, f1).astype(bf16),
        x1,
        *parts,
        *swapped,
    )
    q = ring_zx(q, -1, 0)
    u2 = ring_zx(u2, 0, -1)
    u1 = ring_zx(u1, 0, -1)
    p, o1 = together(add(x1, p).astype(bf16), o1)
    p = ring_zx(p, -1, 0)
    u1, *parts = together(u1, *parts)
    grads = [add(part, other).astype(bf16) for part, other in zip(parts[:2], parts[2:])]
    q = ring_zx(add(o1, q).astype(bf16), -1, 0)
    t = ring_zx(add(h2, u2, d2).astype(bf16), -2, 0)
    p, *grads = together(swap(p), *grads)
    own = add(own, q, p)
    vu, vd, v2, h1 = together(
        own[32:64].astype(bf16), own[64:96].astype(bf16), own[96:].astype(bf16), add(h1, u1, d1)
    )
    s1 = add(h1[32:96], t[:64]).astype(bf16)
    s2 = cat([add(h1[96:128], t[64:]), h1[128:]]).astype(bf16)
    s1 = ring_zx(s1, -1, 0)
    s2 = ring_zx(s2, -2, 0)
    vu = ring_zx(vu, 0, -1)
    vd = ring_zx(vd, 0, 1)
    v2 = ring_zx(v2, 0, -2)
    last = swap(add(s1[32:], s2[32:]).astype(bf16))
    out_a = add(own[:32], vu, vd, v2).astype(bf16)
    out_b = add(h1[:32], s1[:32], s2[:32], last).astype(bf16)
    return out_a, out_b, *grads


def local(kernel, out_shapes, row, *arrays):
    size = 2 * sum(a.size * a.dtype.itemsize for a in arrays)
    return pl.pallas_call(
        kernel,
        out_shape=out_shapes,
        in_specs=[SMEM] + [VMEM] * len(arrays),
        out_specs=jax.tree.map(lambda _: VMEM, out_shapes),
        compiler_params=pltpu.CompilerParams(vmem_limit_bytes=16 * 2**20),
        cost_estimate=pl.CostEstimate(flops=0, bytes_accessed=size, transcendentals=0),
    )(row.reshape(1), *arrays)


CHUNK = jax.ShapeDtypeStruct((256, 384), bf16)


OTHER = (2, 4, 6)


def chunks_a(row, part):
    def kernel(where, ref, *outs):
        for o, out in enumerate(outs):
            x = lax.rem(where[0] + o, NY)
            crossed = jnp.where((x == 1) | (x == 2), 3 - x, x)
            for g in range(8):
                at = pl.multiple_of(128 * g + 32 * (crossed if g in OTHER else x), 32)
                out[32 * g : 32 * (g + 1), :] = ref[pl.ds(at, 32), :]

    return local(kernel, [CHUNK] * 4, row, part)


def chunks_b(row, part):
    def kernel(where, ref, *outs):
        for o, out in enumerate(outs):
            at = pl.multiple_of(lax.rem(where[0] + o, NY) * 256, 256)
            out[...] = ref[pl.ds(at, 256), :]

    return local(kernel, [CHUNK] * 4, row, part)


def join_b(row, parts):
    def kernel(where, *refs):
        for o in range(NY):
            at = pl.multiple_of(lax.rem(where[0] + o, NY) * 256, 256)
            refs[4][pl.ds(at, 256), :] = refs[o][...]

    return local(kernel, jax.ShapeDtypeStruct((1024, 384), bf16), row, *parts)


def join_a(row, parts):
    def kernel(where, *refs):
        for o in range(NY):
            x = lax.rem(where[0] + o, NY)
            crossed = jnp.where((x == 1) | (x == 2), 3 - x, x)
            for g in range(8):
                refs[4][g, crossed if g in OTHER else x] = refs[o][32 * g : 32 * (g + 1), :]

    out = local(kernel, jax.ShapeDtypeStruct((8, 4, 32, 384), bf16), row, *parts)
    return out.reshape(1024, 384)


def scatter_y(at):
    far = shift_y(at[2], 2, -2)
    up = shift_y(at[1], 1, 1)
    down = shift_y(at[3], -1, -1)
    return add(at[0], up, down, far)


def gather_y(mine):
    far = shift_y(mine, 2, -2)
    below = shift_y(mine, 1, 1)
    above = shift_y(mine, -1, -1)
    return [mine, above, far, below]


def dot(left, right, dims):
    return lax.dot_general(left, right, ((dims[:1], dims[1:]), ((), ())), preferred_element_type=f32)


def on_device(tokens, w_in, w_out, cotangent):
    row = lax.axis_index("row")
    cot_rows, tok_rows = gather(cotangent, tokens)
    pre = scatter_y(chunks_b(row, dot(tok_rows, w_in, (1, 0)).astype(bf16)))
    hidden, pre = together(gelu_value(pre).astype(bf16), pre)
    hidden_rows = join_a(row, gather_y(hidden))
    part_mixed = dot(hidden_rows, w_out, (1, 0))
    grad_hidden = scatter_y(chunks_a(row, dot(cot_rows, w_out, (1, 1)).astype(bf16)))
    grad_pre = (grad_hidden * gelu_slope(pre)).astype(bf16)
    pre_grad_rows = join_b(row, gather_y(grad_pre))
    part_tokens = dot(pre_grad_rows, w_in, (1, 1))

    def weight_grads(early):
        hidden_late, pre_grad_late, _ = together(hidden_rows, pre_grad_rows, early)
        return (
            dot(tok_rows, pre_grad_late, (0, 0)).astype(bf16),
            dot(hidden_late, cot_rows, (0, 0)).astype(bf16),
        )

    return scatter(part_mixed, part_tokens, weight_grads)


def solution(mesh):
    placed = (
        P(("depth", "col"), "row"),
        P("row", "depth"),
        P("depth", "row"),
        P(("depth", "col"), "row"),
    )
    return jax.shard_map(
        on_device,
        mesh=mesh,
        in_specs=placed,
        out_specs=(
            P(("depth", "col"), "row"),
            P(("depth", "col"), "row"),
            P("row", "depth"),
            P("depth", "row"),
        ),
        check_vma=False,
    )
```

```python
import jax
import jax.numpy as jnp
from jax import lax
from jax.experimental import pallas as pl
from jax.experimental.pallas import tpu as pltpu
from jax.sharding import PartitionSpec as P

root_half = 0.7071067811865476
inv_root_two_pi = 0.3989422804014327
NZ, NX, NY, NC = 8, 4, 4, 2
bf16 = jnp.bfloat16
f32 = jnp.float32


def gelu_value(pre_act):
    return pre_act * 0.5 * (1.0 + lax.erf(pre_act * root_half))


def gelu_slope(pre_act):
    return (
        0.5 * (1.0 + lax.erf(pre_act * root_half))
        + pre_act * jnp.exp(-0.5 * pre_act * pre_act) * inv_root_two_pi
    )


def shift_zx(value, core0, core1):
    pairs = []
    for z in range(NZ):
        for x in range(NX):
            for c, off in enumerate((core0, core1)):
                if off is not None:
                    to = ((z + off[0]) % NZ) * NX + (x + off[1]) % NX
                    pairs.append(((z * NX + x) * NC + c, to * NC + c))
    return lax.ppermute(value, ("depth", "col"), pairs)


def shift_y(value, core0, core1):
    pairs = []
    for y in range(NY):
        for c, off in enumerate((core0, core1)):
            pairs.append((y * NC + c, ((y + off) % NY) * NC + c))
    return lax.ppermute(value, ("row", "col"), pairs)


def swap(value):
    return lax.ppermute(value, "col", [(0, 1), (1, 0)])


def cat(parts):
    return jnp.concatenate(parts, axis=0)


def add(*terms):
    total = terms[0].astype(f32)
    for t in terms[1:]:
        total = total + t.astype(f32)
    return total


def ring_zx(value, dz, dx):
    return shift_zx(value, (dz, dx), (-dz, -dx))


VMEM = pl.BlockSpec(memory_space=pltpu.VMEM)
SMEM = pl.BlockSpec(memory_space=pltpu.SMEM)


def join(parts):
    arrays = []
    for a, _, _ in parts:
        if not any(a is other for other in arrays):
            arrays.append(a)
    places = [next(i for i, other in enumerate(arrays) if other is a) for a, _, _ in parts]
    rows = sum(t - s for _, s, t in parts)
    width = arrays[0].shape[1]

    def kernel(*refs):
        at = 0
        for i, (_, s, t) in zip(places, parts):
            refs[-1][at : at + t - s, :] = refs[i][s:t, :]
            at += t - s

    return pl.pallas_call(
        kernel,
        out_shape=jax.ShapeDtypeStruct((rows, width), bf16),
        in_specs=[VMEM] * len(arrays),
        out_specs=VMEM,
        compiler_params=pltpu.CompilerParams(vmem_limit_bytes=16 * 2**20),
        cost_estimate=pl.CostEstimate(
            flops=0, bytes_accessed=4 * rows * width, transcendentals=0
        ),
    )(*arrays)


def whole(*arrays):
    return join([(a, 0, a.shape[0]) for a in arrays])


def together(*values):
    return lax.optimization_barrier(values)


def gather(a, b):
    w, a = together(whole(b, swap(b)), a)
    s1 = ring_zx(w, 1, 0)
    s2 = ring_zx(w, 2, 0)
    vu = ring_zx(a, 0, 1)
    vd = ring_zx(a, 0, -1)
    v2 = ring_zx(a, 0, 2)
    own, s1, s2 = together(whole(a, vu, vd, v2), s1, s2)
    so = swap(own)
    o1 = ring_zx(own, 1, 0)
    so, h1, h2 = together(so, whole(b, s1, s2), join([(s1, 0, 64), (s2, 0, 32)]))
    x1 = ring_zx(so, 1, 0)
    o2 = ring_zx(o1, 1, 0)
    u1 = ring_zx(h1, 0, 1)
    d1 = ring_zx(h1, 0, -1)
    h2 = ring_zx(h2, 2, 0)
    x2 = ring_zx(x1, 1, 0)
    o3 = ring_zx(o2, 1, 0)
    f1 = ring_zx(u1, 0, 1)
    u2 = ring_zx(h2, 0, 1)
    d2 = ring_zx(h2, 0, -1)
    x3 = ring_zx(x2, 1, 0)
    o4 = ring_zx(o3, 1, 0)
    f2 = ring_zx(u2, 0, 1)
    return whole(own, o1, x1, o2, x2, o3, x3, o4), whole(h1, h2, u1, u2, d1, d2, f1, f2)


def scatter(part_a, part_b, weight_grads):
    own, o1, x1, o2, x2, o3, x3, o4 = (part_a[128 * j : 128 * (j + 1)] for j in range(8))
    h1, u1, d1, f1 = (part_b[256 * j : 256 * j + 160] for j in range(4))
    h2, u2, d2, f2 = (part_b[256 * j + 160 : 256 * (j + 1)] for j in range(4))
    q = ring_zx(o4.astype(bf16), -1, 0)
    p = ring_zx(x3.astype(bf16), -1, 0)
    f2 = ring_zx(f2.astype(bf16), 0, -1)
    f1 = ring_zx(f1.astype(bf16), 0, -1)
    q, d2, d1, x2 = together(add(o3, q).astype(bf16), d2.astype(bf16), d1.astype(bf16), x2)
    parts = weight_grads(f1)
    swapped = [swap(part) for part in parts]
    q = ring_zx(q, -1, 0)
    d2 = ring_zx(d2, 0, 1)
    d1 = ring_zx(d1, 0, 1)
    p, o2 = together(add(x2, p).astype(bf16), o2)
    p = ring_zx(p, -1, 0)
    q, u2, u1, x1, *parts = together(
        add(o2, q).astype(bf16),
        add(u2, f2).astype(bf16),
        add(u1, f1).astype(bf16),
        x1,
        *parts,
        *swapped,
    )
    q = ring_zx(q, -1, 0)
    u2 = ring_zx(u2, 0, -1)
    u1 = ring_zx(u1, 0, -1)
    p, o1 = together(add(x1, p).astype(bf16), o1)
    p = ring_zx(p, -1, 0)
    u1, *parts = together(u1, *parts)
    grads = [add(part, other).astype(bf16) for part, other in zip(parts[:2], parts[2:])]
    q = ring_zx(add(o1, q).astype(bf16), -1, 0)
    t = ring_zx(add(h2, u2, d2).astype(bf16), -2, 0)
    h1 = add(h1, u1, d1)
    p, s1, s2, *grads = together(
        swap(p),
        add(h1[32:96], t[:64]).astype(bf16),
        cat([add(h1[96:128], t[64:]), h1[128:]]).astype(bf16),
        *grads,
    )
    own = add(own, q, p)
    vu, vd, v2 = own[32:64].astype(bf16), own[64:96].astype(bf16), own[96:].astype(bf16)
    s1 = ring_zx(s1, -1, 0)
    s2 = ring_zx(s2, -2, 0)
    vu = ring_zx(vu, 0, -1)
    vd = ring_zx(vd, 0, 1)
    v2 = ring_zx(v2, 0, -2)
    last = swap(add(s1[32:], s2[32:]).astype(bf16))
    out_a = add(own[:32], vu, vd, v2).astype(bf16)
    out_b = add(h1[:32], s1[:32], s2[:32], last).astype(bf16)
    return out_a, out_b, *grads


def local(kernel, out_shapes, row, *arrays):
    size = 2 * sum(a.size * a.dtype.itemsize for a in arrays)
    return pl.pallas_call(
        kernel,
        out_shape=out_shapes,
        in_specs=[SMEM] + [VMEM] * len(arrays),
        out_specs=jax.tree.map(lambda _: VMEM, out_shapes),
        compiler_params=pltpu.CompilerParams(vmem_limit_bytes=16 * 2**20),
        cost_estimate=pl.CostEstimate(flops=0, bytes_accessed=size, transcendentals=0),
    )(row.reshape(1), *arrays)


CHUNK = jax.ShapeDtypeStruct((256, 384), bf16)


OTHER = (2, 4, 6)


def chunks_a(row, part):
    def kernel(where, ref, *outs):
        for o, out in enumerate(outs):
            x = lax.rem(where[0] + o, NY)
            crossed = jnp.where((x == 1) | (x == 2), 3 - x, x)
            for g in range(8):
                at = pl.multiple_of(128 * g + 32 * (crossed if g in OTHER else x), 32)
                out[32 * g : 32 * (g + 1), :] = ref[pl.ds(at, 32), :]

    return local(kernel, [CHUNK] * 4, row, part)


def chunks_b(row, part):
    def kernel(where, ref, *outs):
        for o, out in enumerate(outs):
            at = pl.multiple_of(lax.rem(where[0] + o, NY) * 256, 256)
            out[...] = ref[pl.ds(at, 256), :]

    return local(kernel, [CHUNK] * 4, row, part)


def join_b(row, parts):
    def kernel(where, *refs):
        for o in range(NY):
            at = pl.multiple_of(lax.rem(where[0] + o, NY) * 256, 256)
            refs[4][pl.ds(at, 256), :] = refs[o][...]

    return local(kernel, jax.ShapeDtypeStruct((1024, 384), bf16), row, *parts)


def join_a(row, parts):
    def kernel(where, *refs):
        for o in range(NY):
            x = lax.rem(where[0] + o, NY)
            crossed = jnp.where((x == 1) | (x == 2), 3 - x, x)
            for g in range(8):
                refs[4][g, crossed if g in OTHER else x] = refs[o][32 * g : 32 * (g + 1), :]

    out = local(kernel, jax.ShapeDtypeStruct((8, 4, 32, 384), bf16), row, *parts)
    return out.reshape(1024, 384)


def scatter_y(at):
    far = shift_y(at[2], 2, -2)
    up = shift_y(at[1], 1, 1)
    down = shift_y(at[3], -1, -1)
    return add(at[0], up, down, far)


def gather_y(mine):
    far = shift_y(mine, 2, -2)
    below = shift_y(mine, 1, 1)
    above = shift_y(mine, -1, -1)
    return [mine, above, far, below]


def dot(left, right, dims):
    return lax.dot_general(left, right, ((dims[:1], dims[1:]), ((), ())), preferred_element_type=f32)


def on_device(tokens, w_in, w_out, cotangent):
    row = lax.axis_index("row")
    cot_rows, tok_rows = gather(cotangent, tokens)
    pre = scatter_y(chunks_b(row, dot(tok_rows, w_in, (1, 0)).astype(bf16)))
    hidden, pre = together(gelu_value(pre).astype(bf16), pre)
    hidden_rows = join_a(row, gather_y(hidden))
    part_mixed = dot(hidden_rows, w_out, (1, 0))
    grad_hidden = scatter_y(chunks_a(row, dot(cot_rows, w_out, (1, 1)).astype(bf16)))
    grad_pre = (grad_hidden * gelu_slope(pre)).astype(bf16)
    pre_grad_rows = join_b(row, gather_y(grad_pre))
    part_tokens = dot(pre_grad_rows, w_in, (1, 1))

    def weight_grads(early):
        hidden_late, pre_grad_late, _ = together(hidden_rows, pre_grad_rows, early)
        return (
            dot(tok_rows, pre_grad_late, (0, 0)).astype(bf16),
            dot(hidden_late, cot_rows, (0, 0)).astype(bf16),
        )

    return scatter(part_mixed, part_tokens, weight_grads)


def solution(mesh):
    placed = (
        P(("depth", "col"), "row"),
        P("row", "depth"),
        P("depth", "row"),
        P(("depth", "col"), "row"),
    )
    return jax.shard_map(
        on_device,
        mesh=mesh,
        in_specs=placed,
        out_specs=(
            P(("depth", "col"), "row"),
            P(("depth", "col"), "row"),
            P("row", "depth"),
            P("depth", "row"),
        ),
        check_vma=False,
    )
```

```python
import jax
import jax.numpy as jnp
from jax import lax
from jax.experimental import pallas as pl
from jax.experimental.pallas import tpu as pltpu
from jax.sharding import PartitionSpec as P

root_half = 0.7071067811865476
inv_root_two_pi = 0.3989422804014327
NZ, NX, NY, NC = 8, 4, 4, 2
bf16 = jnp.bfloat16
f32 = jnp.float32


def gelu_value(pre_act):
    return pre_act * 0.5 * (1.0 + lax.erf(pre_act * root_half))


def gelu_slope(pre_act):
    return (
        0.5 * (1.0 + lax.erf(pre_act * root_half))
        + pre_act * jnp.exp(-0.5 * pre_act * pre_act) * inv_root_two_pi
    )


def shift_zx(value, core0, core1):
    pairs = []
    for z in range(NZ):
        for x in range(NX):
            for c, off in enumerate((core0, core1)):
                if off is not None:
                    to = ((z + off[0]) % NZ) * NX + (x + off[1]) % NX
                    pairs.append(((z * NX + x) * NC + c, to * NC + c))
    return lax.ppermute(value, ("depth", "col"), pairs)


def shift_y(value, core0, core1):
    pairs = []
    for y in range(NY):
        for c, off in enumerate((core0, core1)):
            pairs.append((y * NC + c, ((y + off) % NY) * NC + c))
    return lax.ppermute(value, ("row", "col"), pairs)


def swap(value):
    return lax.ppermute(value, "col", [(0, 1), (1, 0)])


def cat(parts):
    return jnp.concatenate(parts, axis=0)


def add(*terms):
    total = terms[0].astype(f32)
    for t in terms[1:]:
        total = total + t.astype(f32)
    return total


def ring_zx(value, dz, dx):
    return shift_zx(value, (dz, dx), (-dz, -dx))


VMEM = pl.BlockSpec(memory_space=pltpu.VMEM)
SMEM = pl.BlockSpec(memory_space=pltpu.SMEM)


def join(parts):
    arrays = []
    for a, _, _ in parts:
        if not any(a is other for other in arrays):
            arrays.append(a)
    places = [next(i for i, other in enumerate(arrays) if other is a) for a, _, _ in parts]
    rows = sum(t - s for _, s, t in parts)
    width = arrays[0].shape[1]

    def kernel(*refs):
        at = 0
        for i, (_, s, t) in zip(places, parts):
            refs[-1][at : at + t - s, :] = refs[i][s:t, :]
            at += t - s

    return pl.pallas_call(
        kernel,
        out_shape=jax.ShapeDtypeStruct((rows, width), bf16),
        in_specs=[VMEM] * len(arrays),
        out_specs=VMEM,
        compiler_params=pltpu.CompilerParams(vmem_limit_bytes=16 * 2**20),
        cost_estimate=pl.CostEstimate(
            flops=0, bytes_accessed=4 * rows * width, transcendentals=0
        ),
    )(*arrays)


def whole(*arrays):
    return join([(a, 0, a.shape[0]) for a in arrays])


def together(*values):
    return lax.optimization_barrier(values)


def gather(a, b):
    w, a = together(whole(b, swap(b)), a)
    s1 = ring_zx(w, 1, 0)
    s2 = ring_zx(w, 2, 0)
    vu = ring_zx(a, 0, 1)
    vd = ring_zx(a, 0, -1)
    v2 = ring_zx(a, 0, 2)
    own, s1, s2 = together(whole(a, vu, vd, v2), s1, s2)
    so = swap(own)
    o1 = ring_zx(own, 1, 0)
    so, h1, h2 = together(so, whole(b, s1, s2), join([(s1, 0, 64), (s2, 0, 32)]))
    x1 = ring_zx(so, 1, 0)
    o2 = ring_zx(o1, 1, 0)
    u1 = ring_zx(h1, 0, 1)
    d1 = ring_zx(h1, 0, -1)
    h2 = ring_zx(h2, 2, 0)
    x2 = ring_zx(x1, 1, 0)
    o3 = ring_zx(o2, 1, 0)
    f1 = ring_zx(u1, 0, 1)
    u2 = ring_zx(h2, 0, 1)
    d2 = ring_zx(h2, 0, -1)
    x3 = ring_zx(x2, 1, 0)
    o4 = ring_zx(o3, 1, 0)
    f2 = ring_zx(u2, 0, 1)
    return whole(own, o1, x1, o2, x2, o3, x3, o4), whole(h1, h2, u1, u2, d1, d2, f1, f2)


def scatter(part_a, part_b, weight_grads):
    own, o1, x1, o2, x2, o3, x3, o4 = (part_a[128 * j : 128 * (j + 1)] for j in range(8))
    h1, u1, d1, f1 = (part_b[256 * j : 256 * j + 160] for j in range(4))
    h2, u2, d2, f2 = (part_b[256 * j + 160 : 256 * (j + 1)] for j in range(4))
    q = ring_zx(o4.astype(bf16), -1, 0)
    p = ring_zx(x3.astype(bf16), -1, 0)
    f2 = ring_zx(f2.astype(bf16), 0, -1)
    f1 = ring_zx(f1.astype(bf16), 0, -1)
    q, x2 = together(add(o3, q).astype(bf16), x2)
    parts = weight_grads(f1)
    swapped = [swap(part) for part in parts]
    q = ring_zx(q, -1, 0)
    p, o2, d2, d1 = together(add(x2, p).astype(bf16), o2, d2.astype(bf16), d1.astype(bf16))
    p = ring_zx(p, -1, 0)
    d2 = ring_zx(d2, 0, 1)
    d1 = ring_zx(d1, 0, 1)
    q, u2, u1, x1, *parts = together(
        add(o2, q).astype(bf16),
        add(u2, f2).astype(bf16),
        add(u1, f1).astype(bf16),
        x1,
        *parts,
        *swapped,
    )
    q = ring_zx(q, -1, 0)
    u2 = ring_zx(u2, 0, -1)
    u1 = ring_zx(u1, 0, -1)
    p, o1 = together(add(x1, p).astype(bf16), o1)
    p = ring_zx(p, -1, 0)
    u1, *parts = together(u1, *parts)
    grads = [add(part, other).astype(bf16) for part, other in zip(parts[:2], parts[2:])]
    q = ring_zx(add(o1, q).astype(bf16), -1, 0)
    t = ring_zx(add(h2, u2, d2).astype(bf16), -2, 0)
    h1 = add(h1, u1, d1)
    p, s1, s2, *grads = together(
        swap(p),
        add(h1[32:96], t[:64]).astype(bf16),
        cat([add(h1[96:128], t[64:]), h1[128:]]).astype(bf16),
        *grads,
    )
    own = add(own, q, p)
    vu, vd, v2 = own[32:64].astype(bf16), own[64:96].astype(bf16), own[96:].astype(bf16)
    s1 = ring_zx(s1, -1, 0)
    s2 = ring_zx(s2, -2, 0)
    vu = ring_zx(vu, 0, -1)
    vd = ring_zx(vd, 0, 1)
    v2 = ring_zx(v2, 0, -2)
    last = swap(add(s1[32:], s2[32:]).astype(bf16))
    out_a = add(own[:32], vu, vd, v2).astype(bf16)
    out_b = add(h1[:32], s1[:32], s2[:32], last).astype(bf16)
    return out_a, out_b, *grads


def local(kernel, out_shapes, row, *arrays):
    size = 2 * sum(a.size * a.dtype.itemsize for a in arrays)
    return pl.pallas_call(
        kernel,
        out_shape=out_shapes,
        in_specs=[SMEM] + [VMEM] * len(arrays),
        out_specs=jax.tree.map(lambda _: VMEM, out_shapes),
        compiler_params=pltpu.CompilerParams(vmem_limit_bytes=16 * 2**20),
        cost_estimate=pl.CostEstimate(flops=0, bytes_accessed=size, transcendentals=0),
    )(row.reshape(1), *arrays)


CHUNK = jax.ShapeDtypeStruct((256, 384), bf16)


OTHER = (2, 4, 6)


def chunks_a(row, part):
    def kernel(where, ref, *outs):
        for o, out in enumerate(outs):
            x = lax.rem(where[0] + o, NY)
            crossed = jnp.where((x == 1) | (x == 2), 3 - x, x)
            for g in range(8):
                at = pl.multiple_of(128 * g + 32 * (crossed if g in OTHER else x), 32)
                out[32 * g : 32 * (g + 1), :] = ref[pl.ds(at, 32), :]

    return local(kernel, [CHUNK] * 4, row, part)


def chunks_b(row, part):
    def kernel(where, ref, *outs):
        for o, out in enumerate(outs):
            at = pl.multiple_of(lax.rem(where[0] + o, NY) * 256, 256)
            out[...] = ref[pl.ds(at, 256), :]

    return local(kernel, [CHUNK] * 4, row, part)


def join_b(row, parts):
    def kernel(where, *refs):
        for o in range(NY):
            at = pl.multiple_of(lax.rem(where[0] + o, NY) * 256, 256)
            refs[4][pl.ds(at, 256), :] = refs[o][...]

    return local(kernel, jax.ShapeDtypeStruct((1024, 384), bf16), row, *parts)


def join_a(row, parts):
    def kernel(where, *refs):
        for o in range(NY):
            x = lax.rem(where[0] + o, NY)
            crossed = jnp.where((x == 1) | (x == 2), 3 - x, x)
            for g in range(8):
                refs[4][g, crossed if g in OTHER else x] = refs[o][32 * g : 32 * (g + 1), :]

    out = local(kernel, jax.ShapeDtypeStruct((8, 4, 32, 384), bf16), row, *parts)
    return out.reshape(1024, 384)


def scatter_y(at):
    far = shift_y(at[2], 2, -2)
    up = shift_y(at[1], 1, 1)
    down = shift_y(at[3], -1, -1)
    return add(at[0], up, down, far)


def gather_y(mine):
    far = shift_y(mine, 2, -2)
    below = shift_y(mine, 1, 1)
    above = shift_y(mine, -1, -1)
    return [mine, above, far, below]


def dot(left, right, dims):
    return lax.dot_general(left, right, ((dims[:1], dims[1:]), ((), ())), preferred_element_type=f32)


def on_device(tokens, w_in, w_out, cotangent):
    row = lax.axis_index("row")
    cot_rows, tok_rows = gather(cotangent, tokens)
    pre = scatter_y(chunks_b(row, dot(tok_rows, w_in, (1, 0)).astype(bf16)))
    hidden, pre = together(gelu_value(pre).astype(bf16), pre)
    hidden_rows = join_a(row, gather_y(hidden))
    part_mixed = dot(hidden_rows, w_out, (1, 0))
    grad_hidden = scatter_y(chunks_a(row, dot(cot_rows, w_out, (1, 1)).astype(bf16)))
    grad_pre = (grad_hidden * gelu_slope(pre)).astype(bf16)
    pre_grad_rows = join_b(row, gather_y(grad_pre))
    part_tokens = dot(pre_grad_rows, w_in, (1, 1))

    def weight_grads(early):
        hidden_late, pre_grad_late, _ = together(hidden_rows, pre_grad_rows, early)
        return (
            dot(tok_rows, pre_grad_late, (0, 0)).astype(bf16),
            dot(hidden_late, cot_rows, (0, 0)).astype(bf16),
        )

    return scatter(part_mixed, part_tokens, weight_grads)


def solution(mesh):
    placed = (
        P(("depth", "col"), "row"),
        P("row", "depth"),
        P("depth", "row"),
        P(("depth", "col"), "row"),
    )
    return jax.shard_map(
        on_device,
        mesh=mesh,
        in_specs=placed,
        out_specs=(
            P(("depth", "col"), "row"),
            P(("depth", "col"), "row"),
            P("row", "depth"),
            P("depth", "row"),
        ),
        check_vma=False,
    )
```

```python
import jax
import jax.numpy as jnp
from jax import lax
from jax.experimental import pallas as pl
from jax.experimental.pallas import tpu as pltpu
from jax.sharding import PartitionSpec as P

root_half = 0.7071067811865476
inv_root_two_pi = 0.3989422804014327
NZ, NX, NY, NC = 8, 4, 4, 2
bf16 = jnp.bfloat16
f32 = jnp.float32


def gelu_value(pre_act):
    return pre_act * 0.5 * (1.0 + lax.erf(pre_act * root_half))


def gelu_slope(pre_act):
    return (
        0.5 * (1.0 + lax.erf(pre_act * root_half))
        + pre_act * jnp.exp(-0.5 * pre_act * pre_act) * inv_root_two_pi
    )


def shift_zx(value, core0, core1):
    pairs = []
    for z in range(NZ):
        for x in range(NX):
            for c, off in enumerate((core0, core1)):
                if off is not None:
                    to = ((z + off[0]) % NZ) * NX + (x + off[1]) % NX
                    pairs.append(((z * NX + x) * NC + c, to * NC + c))
    return lax.ppermute(value, ("depth", "col"), pairs)


def shift_y(value, core0, core1):
    pairs = []
    for y in range(NY):
        for c, off in enumerate((core0, core1)):
            pairs.append((y * NC + c, ((y + off) % NY) * NC + c))
    return lax.ppermute(value, ("row", "col"), pairs)


def swap(value):
    return lax.ppermute(value, "col", [(0, 1), (1, 0)])


def cat(parts):
    return jnp.concatenate(parts, axis=0)


def add(*terms):
    total = terms[0].astype(f32)
    for t in terms[1:]:
        total = total + t.astype(f32)
    return total


def ring_zx(value, dz, dx):
    return shift_zx(value, (dz, dx), (-dz, -dx))


VMEM = pl.BlockSpec(memory_space=pltpu.VMEM)
SMEM = pl.BlockSpec(memory_space=pltpu.SMEM)


def join(parts):
    arrays = []
    for a, _, _ in parts:
        if not any(a is other for other in arrays):
            arrays.append(a)
    places = [next(i for i, other in enumerate(arrays) if other is a) for a, _, _ in parts]
    rows = sum(t - s for _, s, t in parts)
    width = arrays[0].shape[1]

    def kernel(*refs):
        at = 0
        for i, (_, s, t) in zip(places, parts):
            refs[-1][at : at + t - s, :] = refs[i][s:t, :]
            at += t - s

    return pl.pallas_call(
        kernel,
        out_shape=jax.ShapeDtypeStruct((rows, width), bf16),
        in_specs=[VMEM] * len(arrays),
        out_specs=VMEM,
        compiler_params=pltpu.CompilerParams(vmem_limit_bytes=16 * 2**20),
        cost_estimate=pl.CostEstimate(
            flops=0, bytes_accessed=4 * rows * width, transcendentals=0
        ),
    )(*arrays)


def whole(*arrays):
    return join([(a, 0, a.shape[0]) for a in arrays])


def together(*values):
    return lax.optimization_barrier(values)


def gather(a, b):
    w, a = together(whole(b, swap(b)), a)
    s1 = ring_zx(w, 1, 0)
    s2 = ring_zx(w, 2, 0)
    vu = ring_zx(a, 0, 1)
    vd = ring_zx(a, 0, -1)
    v2 = ring_zx(a, 0, 2)
    own, s1, s2 = together(whole(a, vu, vd, v2), s1, s2)
    so = swap(own)
    o1 = ring_zx(own, 1, 0)
    so, h1, h2 = together(so, whole(b, s1, s2), join([(s1, 0, 64), (s2, 0, 32)]))
    x1 = ring_zx(so, 1, 0)
    o2 = ring_zx(o1, 1, 0)
    u1 = ring_zx(h1, 0, 1)
    d1 = ring_zx(h1, 0, -1)
    h2 = ring_zx(h2, 2, 0)
    x2 = ring_zx(x1, 1, 0)
    o3 = ring_zx(o2, 1, 0)
    f1 = ring_zx(u1, 0, 1)
    u2 = ring_zx(h2, 0, 1)
    d2 = ring_zx(h2, 0, -1)
    x3 = ring_zx(x2, 1, 0)
    o4 = ring_zx(o3, 1, 0)
    f2 = ring_zx(u2, 0, 1)
    return whole(own, o1, x1, o2, x2, o3, x3, o4), whole(h1, h2, u1, u2, d1, d2, f1, f2)


def scatter(part_a, part_b, weight_grads):
    own, o1, x1, o2, x2, o3, x3, o4 = (part_a[128 * j : 128 * (j + 1)] for j in range(8))
    h1, u1, d1, f1 = (part_b[256 * j : 256 * j + 160] for j in range(4))
    h2, u2, d2, f2 = (part_b[256 * j + 160 : 256 * (j + 1)] for j in range(4))
    q = ring_zx(o4.astype(bf16), -1, 0)
    p = ring_zx(x3.astype(bf16), -1, 0)
    f2 = ring_zx(f2.astype(bf16), 0, -1)
    f1 = ring_zx(f1.astype(bf16), 0, -1)
    q, x2 = together(add(o3, q).astype(bf16), x2)
    parts = weight_grads(f2)
    swapped = [swap(part) for part in parts]
    q = ring_zx(q, -1, 0)
    p, o2, d2, d1 = together(add(x2, p).astype(bf16), o2, d2.astype(bf16), d1.astype(bf16))
    p = ring_zx(p, -1, 0)
    d2 = ring_zx(d2, 0, 1)
    d1 = ring_zx(d1, 0, 1)
    q, x1, *parts = together(add(o2, q).astype(bf16), x1, *parts)
    q = ring_zx(q, -1, 0)
    p, o1, u2, u1, *parts = together(
        add(x1, p).astype(bf16),
        o1,
        add(u2, f2).astype(bf16),
        add(u1, f1).astype(bf16),
        *parts,
        *swapped,
    )
    u2 = ring_zx(u2, 0, -1)
    u1 = ring_zx(u1, 0, -1)
    p = ring_zx(p, -1, 0)
    u1, *parts = together(u1, *parts)
    grads = [add(part, other).astype(bf16) for part, other in zip(parts[:2], parts[2:])]
    q = ring_zx(add(o1, q).astype(bf16), -1, 0)
    t = ring_zx(add(h2, u2, d2).astype(bf16), -2, 0)
    h1 = add(h1, u1, d1)
    p, s1, s2, *grads = together(
        swap(p),
        add(h1[32:96], t[:64]).astype(bf16),
        cat([add(h1[96:128], t[64:]), h1[128:]]).astype(bf16),
        *grads,
    )
    own = add(own, q, p)
    vu, vd, v2 = own[32:64].astype(bf16), own[64:96].astype(bf16), own[96:].astype(bf16)
    s1 = ring_zx(s1, -1, 0)
    s2 = ring_zx(s2, -2, 0)
    vu = ring_zx(vu, 0, -1)
    vd = ring_zx(vd, 0, 1)
    v2 = ring_zx(v2, 0, -2)
    last = swap(add(s1[32:], s2[32:]).astype(bf16))
    out_a = add(own[:32], vu, vd, v2).astype(bf16)
    out_b = add(h1[:32], s1[:32], s2[:32], last).astype(bf16)
    return out_a, out_b, *grads


def local(kernel, out_shapes, row, *arrays):
    size = 2 * sum(a.size * a.dtype.itemsize for a in arrays)
    return pl.pallas_call(
        kernel,
        out_shape=out_shapes,
        in_specs=[SMEM] + [VMEM] * len(arrays),
        out_specs=jax.tree.map(lambda _: VMEM, out_shapes),
        compiler_params=pltpu.CompilerParams(vmem_limit_bytes=16 * 2**20),
        cost_estimate=pl.CostEstimate(flops=0, bytes_accessed=size, transcendentals=0),
    )(row.reshape(1), *arrays)


CHUNK = jax.ShapeDtypeStruct((256, 384), bf16)


OTHER = (2, 4, 6)


def chunks_a(row, part):
    def kernel(where, ref, *outs):
        for o, out in enumerate(outs):
            x = lax.rem(where[0] + o, NY)
            crossed = jnp.where((x == 1) | (x == 2), 3 - x, x)
            for g in range(8):
                at = pl.multiple_of(128 * g + 32 * (crossed if g in OTHER else x), 32)
                out[32 * g : 32 * (g + 1), :] = ref[pl.ds(at, 32), :]

    return local(kernel, [CHUNK] * 4, row, part)


def chunks_b(row, part):
    def kernel(where, ref, *outs):
        for o, out in enumerate(outs):
            at = pl.multiple_of(lax.rem(where[0] + o, NY) * 256, 256)
            out[...] = ref[pl.ds(at, 256), :]

    return local(kernel, [CHUNK] * 4, row, part)


def join_b(row, parts):
    def kernel(where, *refs):
        for o in range(NY):
            at = pl.multiple_of(lax.rem(where[0] + o, NY) * 256, 256)
            refs[4][pl.ds(at, 256), :] = refs[o][...]

    return local(kernel, jax.ShapeDtypeStruct((1024, 384), bf16), row, *parts)


def join_a(row, parts):
    def kernel(where, *refs):
        for o in range(NY):
            x = lax.rem(where[0] + o, NY)
            crossed = jnp.where((x == 1) | (x == 2), 3 - x, x)
            for g in range(8):
                refs[4][g, crossed if g in OTHER else x] = refs[o][32 * g : 32 * (g + 1), :]

    out = local(kernel, jax.ShapeDtypeStruct((8, 4, 32, 384), bf16), row, *parts)
    return out.reshape(1024, 384)


def scatter_y(at):
    far = shift_y(at[2], 2, -2)
    up = shift_y(at[1], 1, 1)
    down = shift_y(at[3], -1, -1)
    return add(at[0], up, down, far)


def gather_y(mine):
    far = shift_y(mine, 2, -2)
    below = shift_y(mine, 1, 1)
    above = shift_y(mine, -1, -1)
    return [mine, above, far, below]


def dot(left, right, dims):
    return lax.dot_general(left, right, ((dims[:1], dims[1:]), ((), ())), preferred_element_type=f32)


def on_device(tokens, w_in, w_out, cotangent):
    row = lax.axis_index("row")
    cot_rows, tok_rows = gather(cotangent, tokens)
    pre = scatter_y(chunks_b(row, dot(tok_rows, w_in, (1, 0)).astype(bf16)))
    hidden, pre = together(gelu_value(pre).astype(bf16), pre)
    hidden_rows = join_a(row, gather_y(hidden))
    part_mixed = dot(hidden_rows, w_out, (1, 0))
    grad_hidden = scatter_y(chunks_a(row, dot(cot_rows, w_out, (1, 1)).astype(bf16)))
    grad_pre = (grad_hidden * gelu_slope(pre)).astype(bf16)
    pre_grad_rows = join_b(row, gather_y(grad_pre))
    part_tokens = dot(pre_grad_rows, w_in, (1, 1))

    def weight_grads(early):
        hidden_late, pre_grad_late, _ = together(hidden_rows, pre_grad_rows, early)
        return (
            dot(tok_rows, pre_grad_late, (0, 0)).astype(bf16),
            dot(hidden_late, cot_rows, (0, 0)).astype(bf16),
        )

    return scatter(part_mixed, part_tokens, weight_grads)


def solution(mesh):
    placed = (
        P(("depth", "col"), "row"),
        P("row", "depth"),
        P("depth", "row"),
        P(("depth", "col"), "row"),
    )
    return jax.shard_map(
        on_device,
        mesh=mesh,
        in_specs=placed,
        out_specs=(
            P(("depth", "col"), "row"),
            P(("depth", "col"), "row"),
            P("row", "depth"),
            P("depth", "row"),
        ),
        check_vma=False,
    )
```

```python
import jax
import jax.numpy as jnp
from jax import lax
from jax.experimental import pallas as pl
from jax.experimental.pallas import tpu as pltpu
from jax.sharding import PartitionSpec as P

root_half = 0.7071067811865476
inv_root_two_pi = 0.3989422804014327
NZ, NX, NY, NC = 8, 4, 4, 2
bf16 = jnp.bfloat16
f32 = jnp.float32


def gelu_value(pre_act):
    return pre_act * 0.5 * (1.0 + lax.erf(pre_act * root_half))


def gelu_slope(pre_act):
    return (
        0.5 * (1.0 + lax.erf(pre_act * root_half))
        + pre_act * jnp.exp(-0.5 * pre_act * pre_act) * inv_root_two_pi
    )


def shift_zx(value, core0, core1):
    pairs = []
    for z in range(NZ):
        for x in range(NX):
            for c, off in enumerate((core0, core1)):
                if off is not None:
                    to = ((z + off[0]) % NZ) * NX + (x + off[1]) % NX
                    pairs.append(((z * NX + x) * NC + c, to * NC + c))
    return lax.ppermute(value, ("depth", "col"), pairs)


def shift_y(value, core0, core1):
    pairs = []
    for y in range(NY):
        for c, off in enumerate((core0, core1)):
            pairs.append((y * NC + c, ((y + off) % NY) * NC + c))
    return lax.ppermute(value, ("row", "col"), pairs)


def swap(value):
    return lax.ppermute(value, "col", [(0, 1), (1, 0)])


def cat(parts):
    return jnp.concatenate(parts, axis=0)


def add(*terms):
    total = terms[0].astype(f32)
    for t in terms[1:]:
        total = total + t.astype(f32)
    return total


def ring_zx(value, dz, dx):
    return shift_zx(value, (dz, dx), (-dz, -dx))


VMEM = pl.BlockSpec(memory_space=pltpu.VMEM)
SMEM = pl.BlockSpec(memory_space=pltpu.SMEM)


def join(parts):
    arrays = []
    for a, _, _ in parts:
        if not any(a is other for other in arrays):
            arrays.append(a)
    places = [next(i for i, other in enumerate(arrays) if other is a) for a, _, _ in parts]
    rows = sum(t - s for _, s, t in parts)
    width = arrays[0].shape[1]

    def kernel(*refs):
        at = 0
        for i, (_, s, t) in zip(places, parts):
            refs[-1][at : at + t - s, :] = refs[i][s:t, :]
            at += t - s

    return pl.pallas_call(
        kernel,
        out_shape=jax.ShapeDtypeStruct((rows, width), bf16),
        in_specs=[VMEM] * len(arrays),
        out_specs=VMEM,
        compiler_params=pltpu.CompilerParams(vmem_limit_bytes=16 * 2**20),
        cost_estimate=pl.CostEstimate(
            flops=0, bytes_accessed=4 * rows * width, transcendentals=0
        ),
    )(*arrays)


def whole(*arrays):
    return join([(a, 0, a.shape[0]) for a in arrays])


def together(*values):
    return lax.optimization_barrier(values)


def gather(a, b):
    w, a = together(whole(b, swap(b)), a)
    s1 = ring_zx(w, 1, 0)
    s2 = ring_zx(w, 2, 0)
    vu = ring_zx(a, 0, 1)
    vd = ring_zx(a, 0, -1)
    v2 = ring_zx(a, 0, 2)
    own, s1, s2 = together(whole(a, vu, vd, v2), s1, s2)
    so = swap(own)
    o1 = ring_zx(own, 1, 0)
    so, h1, h2 = together(so, whole(b, s1, s2), join([(s1, 0, 64), (s2, 0, 32)]))
    x1 = ring_zx(so, 1, 0)
    o2 = ring_zx(o1, 1, 0)
    u1 = ring_zx(h1, 0, 1)
    d1 = ring_zx(h1, 0, -1)
    h2 = ring_zx(h2, 2, 0)
    x2 = ring_zx(x1, 1, 0)
    o3 = ring_zx(o2, 1, 0)
    f1 = ring_zx(u1, 0, 1)
    u2 = ring_zx(h2, 0, 1)
    d2 = ring_zx(h2, 0, -1)
    x3 = ring_zx(x2, 1, 0)
    o4 = ring_zx(o3, 1, 0)
    f2 = ring_zx(u2, 0, 1)
    return whole(own, o1, x1, o2, x2, o3, x3, o4), whole(h1, h2, u1, u2, d1, d2, f1, f2)


def scatter(part_a, part_b, weight_grads):
    own, o1, x1, o2, x2, o3, x3, o4 = (part_a[128 * j : 128 * (j + 1)] for j in range(8))
    h1, u1, d1, f1 = (part_b[256 * j : 256 * j + 160] for j in range(4))
    h2, u2, d2, f2 = (part_b[256 * j + 160 : 256 * (j + 1)] for j in range(4))
    q = ring_zx(o4.astype(bf16), -1, 0)
    p = ring_zx(x3.astype(bf16), -1, 0)
    f2 = ring_zx(f2.astype(bf16), 0, -1)
    f1 = ring_zx(f1.astype(bf16), 0, -1)
    q, x2 = together(add(o3, q).astype(bf16), x2)
    parts = weight_grads(f2)
    swapped = [swap(part) for part in parts]
    q = ring_zx(q, -1, 0)
    p, o2, d2, d1 = together(add(x2, p).astype(bf16), o2, d2.astype(bf16), d1.astype(bf16))
    p = ring_zx(p, -1, 0)
    d2 = ring_zx(d2, 0, 1)
    d1 = ring_zx(d1, 0, 1)
    q, u2, x1, *parts = together(
        add(o2, q).astype(bf16), add(u2, f2).astype(bf16), x1, *parts
    )
    q = ring_zx(q, -1, 0)
    u2 = ring_zx(u2, 0, -1)
    p, o1, u1, *parts = together(
        add(x1, p).astype(bf16), o1, add(u1, f1).astype(bf16), *parts, *swapped
    )
    p = ring_zx(p, -1, 0)
    u1 = ring_zx(u1, 0, -1)
    u1, *parts = together(u1, *parts)
    grads = [add(part, other).astype(bf16) for part, other in zip(parts[:2], parts[2:])]
    q = ring_zx(add(o1, q).astype(bf16), -1, 0)
    t = ring_zx(add(h2, u2, d2).astype(bf16), -2, 0)
    h1 = add(h1, u1, d1)
    p, s1, s2, *grads = together(
        swap(p),
        add(h1[32:96], t[:64]).astype(bf16),
        cat([add(h1[96:128], t[64:]), h1[128:]]).astype(bf16),
        *grads,
    )
    own = add(own, q, p)
    vu, vd, v2 = own[32:64].astype(bf16), own[64:96].astype(bf16), own[96:].astype(bf16)
    s1 = ring_zx(s1, -1, 0)
    s2 = ring_zx(s2, -2, 0)
    vu = ring_zx(vu, 0, -1)
    vd = ring_zx(vd, 0, 1)
    v2 = ring_zx(v2, 0, -2)
    last = swap(add(s1[32:], s2[32:]).astype(bf16))
    out_a = add(own[:32], vu, vd, v2).astype(bf16)
    out_b = add(h1[:32], s1[:32], s2[:32], last).astype(bf16)
    return out_a, out_b, *grads


def local(kernel, out_shapes, row, *arrays):
    size = 2 * sum(a.size * a.dtype.itemsize for a in arrays)
    return pl.pallas_call(
        kernel,
        out_shape=out_shapes,
        in_specs=[SMEM] + [VMEM] * len(arrays),
        out_specs=jax.tree.map(lambda _: VMEM, out_shapes),
        compiler_params=pltpu.CompilerParams(vmem_limit_bytes=16 * 2**20),
        cost_estimate=pl.CostEstimate(flops=0, bytes_accessed=size, transcendentals=0),
    )(row.reshape(1), *arrays)


CHUNK = jax.ShapeDtypeStruct((256, 384), bf16)


OTHER = (2, 4, 6)


def chunks_a(row, part):
    def kernel(where, ref, *outs):
        for o, out in enumerate(outs):
            x = lax.rem(where[0] + o, NY)
            crossed = jnp.where((x == 1) | (x == 2), 3 - x, x)
            for g in range(8):
                at = pl.multiple_of(128 * g + 32 * (crossed if g in OTHER else x), 32)
                out[32 * g : 32 * (g + 1), :] = ref[pl.ds(at, 32), :]

    return local(kernel, [CHUNK] * 4, row, part)


def chunks_b(row, part):
    def kernel(where, ref, *outs):
        for o, out in enumerate(outs):
            at = pl.multiple_of(lax.rem(where[0] + o, NY) * 256, 256)
            out[...] = ref[pl.ds(at, 256), :]

    return local(kernel, [CHUNK] * 4, row, part)


def join_b(row, parts):
    def kernel(where, *refs):
        for o in range(NY):
            at = pl.multiple_of(lax.rem(where[0] + o, NY) * 256, 256)
            refs[4][pl.ds(at, 256), :] = refs[o][...]

    return local(kernel, jax.ShapeDtypeStruct((1024, 384), bf16), row, *parts)


def join_a(row, parts):
    def kernel(where, *refs):
        for o in range(NY):
            x = lax.rem(where[0] + o, NY)
            crossed = jnp.where((x == 1) | (x == 2), 3 - x, x)
            for g in range(8):
                refs[4][g, crossed if g in OTHER else x] = refs[o][32 * g : 32 * (g + 1), :]

    out = local(kernel, jax.ShapeDtypeStruct((8, 4, 32, 384), bf16), row, *parts)
    return out.reshape(1024, 384)


def scatter_y(at):
    far = shift_y(at[2], 2, -2)
    up = shift_y(at[1], 1, 1)
    down = shift_y(at[3], -1, -1)
    return add(at[0], up, down, far)


def gather_y(mine):
    far = shift_y(mine, 2, -2)
    below = shift_y(mine, 1, 1)
    above = shift_y(mine, -1, -1)
    return [mine, above, far, below]


def dot(left, right, dims):
    return lax.dot_general(left, right, ((dims[:1], dims[1:]), ((), ())), preferred_element_type=f32)


def on_device(tokens, w_in, w_out, cotangent):
    row = lax.axis_index("row")
    cot_rows, tok_rows = gather(cotangent, tokens)
    pre = scatter_y(chunks_b(row, dot(tok_rows, w_in, (1, 0)).astype(bf16)))
    hidden, pre = together(gelu_value(pre).astype(bf16), pre)
    hidden_rows = join_a(row, gather_y(hidden))
    part_mixed = dot(hidden_rows, w_out, (1, 0))
    grad_hidden = scatter_y(chunks_a(row, dot(cot_rows, w_out, (1, 1)).astype(bf16)))
    grad_pre = (grad_hidden * gelu_slope(pre)).astype(bf16)
    pre_grad_rows = join_b(row, gather_y(grad_pre))
    part_tokens = dot(pre_grad_rows, w_in, (1, 1))

    def weight_grads(early):
        hidden_late, pre_grad_late, _ = together(hidden_rows, pre_grad_rows, early)
        return (
            dot(tok_rows, pre_grad_late, (0, 0)).astype(bf16),
            dot(hidden_late, cot_rows, (0, 0)).astype(bf16),
        )

    return scatter(part_mixed, part_tokens, weight_grads)


def solution(mesh):
    placed = (
        P(("depth", "col"), "row"),
        P("row", "depth"),
        P("depth", "row"),
        P(("depth", "col"), "row"),
    )
    return jax.shard_map(
        on_device,
        mesh=mesh,
        in_specs=placed,
        out_specs=(
            P(("depth", "col"), "row"),
            P(("depth", "col"), "row"),
            P("row", "depth"),
            P("depth", "row"),
        ),
        check_vma=False,
    )
```
